128 devices in a mesh: seq: 16 (over x, y), enc: 8 (over z, core).
Axes of the slice: x: 4, y: 4, z: 4, core: 2. Of those that a mesh axis runs over, the one named last changes fastest.
Arguments:
- queries: bfloat16 [8192, 4096], P('seq', 'enc'), may hold values from -288 to 288
- out_grad: bfloat16 [8192, 4096], P('seq', 'enc'), may hold values from -48 to 48
- enc_table: bfloat16 [1024, 896, 128], P('seq', 'enc'), may hold values from -6 to 6
- key_weight: bfloat16 [896, 4096], P(None, 'enc'), may hold values from -0.1875 to 0.1875
- value_weight: bfloat16 [896, 4096], P(None, 'enc'), may hold values from -0.1875 to 0.1875
- neighbour_owner: int32 [128, 2], P('seq'), may hold values from 0 to 15, all different within a row; in each aligned block of 8 rows (0 to 7, 8 to 15, ...) at most 2 rows name the same one
- neighbour_row: int32 [128, 2], P('seq'), may hold values from 0 to 63
Outputs:
- d_query: bfloat16 [8192, 4096], P('seq', 'enc')
- d_table: float32 [1024, 896, 128], P('seq', 'enc')
The draws below stay inside these ranges and needn't reach their ends.
Inputs may be any that keep to these rules, and one draw needn't show every extreme that they name: `neighbour_owner`: the 2 neighbours of a span have different owners. Among the 8 rows of one index of seq, no owner is named more than 2 times, a bound that some block reaches.
All inputs are finite; a program needn't handle non-finite values.
Results may differ from the reference program's by a relative error of at most 0.025.
The reference program's roundings to bfloat16 on the way count: a program that leaves them out, or rounds other values in their place, can miss the bound.
Values may be sent and summed in bfloat16 or wider, within the bound.
A program may use at most 128 MiB of HBM per device.

```python
import math
import jax
import jax.numpy as jnp
import numpy as np
from jax import lax

M = 64
KN = 2
R = 128
DE = 896
HEADS = 32
DH = 128
CH_DEV = 8
BLK_DEV = 64
SEQ_LEN = 2048
TOKENS = 8192
SPANS = 128
NBLK = 1024
CAP = 2
N_SEQ = 16


def draw_queries(key, part):
    key = jax.random.fold_in(key, 11)
    base = jax.random.truncated_normal(key, -6.0, 6.0, (TOKENS, HEADS * DH), jnp.float32)
    return base.astype(jnp.bfloat16)


def place_ends(drawn, key, least, high):
    longest = drawn.shape.index(max(drawn.shape))
    spots = []
    for shift in (0, 1):
        where = [jax.random.randint(jax.random.fold_in(key, axis), (), 0, length) for axis, length in enumerate(drawn.shape)]
        where[longest] = (where[longest] + shift) % drawn.shape[longest]
        spots.append(tuple(where))
    return drawn.at[spots[0]].set(least).at[spots[1]].set(high)


def block_levels(own_key, shape, split, least, high):
    def one(dim, blocks):
        steps = jax.random.uniform(jax.random.fold_in(jax.random.fold_in(own_key, 6), dim), (blocks,), jnp.float32, least / len(split), high / len(split))
        return jnp.repeat(jnp.exp(steps), shape[dim] // blocks).reshape((-1,) + (1,) * (len(shape) - dim - 1))

    gain = one(*split[0])
    for cut in split[1:]:
        gain = gain * one(*cut)
    return gain


def shared_out(rng, own, number, rows, number_of, top, reach, slope):
    ranking = jax.random.permutation(rng, number_of)
    heavy_load, usual = portions_of(number_of, rows * top, reach, slope, True), portions_of(number_of, rows * top, reach, slope, False)
    places = jnp.arange(number_of)

    def named(tallies, turn):
        used = int((tallies > 0).sum())
        fixed = max(1, used // 4)
        passed = fixed + (places - fixed + turn * (used - fixed)) % max(1, number_of - fixed)
        return jnp.zeros((number_of,), jnp.int32).at[ranking[jnp.where(places < fixed, places, passed)]].set(jnp.asarray(tallies, jnp.int32))

    tallies = jnp.where(number % 4 == 0, named(heavy_load, number // 4), named(usual, number - number // 4 - 1))
    mixed = jax.random.permutation(jax.random.fold_in(own, 3), number_of)
    giver, receiver = mixed[0:number_of // 2 * 2:2], mixed[1:number_of // 2 * 2:2]
    slack = jnp.minimum(tallies[giver] - 1, reach - tallies[receiver]) // 2
    slack = jnp.where((giver == ranking[0]) | (receiver == ranking[0]) | (tallies[receiver] == 0), 0, jnp.maximum(slack, 0))
    passed = jax.random.randint(jax.random.fold_in(own, 4), (number_of // 2,), 0, 1 << 20) % (slack + 1)
    tallies = tallies.at[giver].add(-passed).at[receiver].add(passed)
    labels = jnp.searchsorted(jnp.cumsum(tallies), jnp.arange(rows * top), side="right").astype(jnp.int32)
    listing = labels.reshape(top, rows).T
    listing = listing[jax.random.permutation(jax.random.fold_in(own, 1), rows)]
    turn = jax.random.randint(jax.random.fold_in(own, 2), (rows, 1), 0, top)
    return jnp.take_along_axis(listing, (jnp.arange(top)[None, :] + turn) % top, axis=1)


def portions_of(count, total, limit, slope, full):
    portions = [(1 << 20) // math.isqrt(rank ** slope) + 1 for rank in range(1, count + 1)]
    largest = limit if full else min(limit, max(-(-total // count), total * portions[0] // sum(portions)))
    least = 1 if total - largest >= count - 1 else 0
    holding, surplus = [largest] + [least] * (count - 1), total - largest - least * (count - 1)
    while surplus > 0:
        free = [i for i in range(1, count) if holding[i] < largest] or [i for i in range(1, count) if holding[i] < limit]
        pool, left = sum([portions[i] for i in free]), surplus
        for i in free:
            more = min(limit - holding[i], max(1, left * portions[i] // pool), surplus)
            holding[i] = holding[i] + more
            surplus = surplus - more
    return np.array(holding)


def scatter_about(stream_key, dims, width, reach, pieces=(), dtype=jnp.bfloat16):
    array = width * jax.random.normal(stream_key, dims, jnp.float32)
    if pieces:
        array = array * block_levels(stream_key, dims, pieces, -0.22, 0.18)
    return jnp.clip(array, -reach, reach).astype(dtype)


def setup_inputs(seed: int = 0) -> dict:
    streams_of = jax.random.split(jax.random.key(seed), 8)
    queries = draw_queries(jax.random.fold_in(streams_of[7], 71), 0)
    out_grad = scatter_about(streams_of[1], (TOKENS, HEADS * DH), 8.0, 48.0, ((0, 16), (1, 8)))
    enc_table = scatter_about(streams_of[2], (NBLK, DE, R), 1.0, 6.0, ((0, 16), (1, 8)))
    key_weight = scatter_about(streams_of[3], (DE, HEADS * DH), DE ** -0.5, 0.1875, ((1, 8),))
    value_weight = scatter_about(streams_of[4], (DE, HEADS * DH), DE ** -0.5, 0.1875, ((1, 8),))
    neighbour_owner_keys = jax.random.split(jax.random.fold_in(streams_of[5], 1), SPANS // CH_DEV)
    neighbour_owner_turns = jax.random.permutation(jax.random.fold_in(streams_of[5], 3), SPANS // CH_DEV)
    neighbour_owner = jax.vmap(lambda own, number: shared_out(jax.random.fold_in(streams_of[5], 2), own, number, CH_DEV, N_SEQ, KN, CAP, 2))(neighbour_owner_keys, neighbour_owner_turns).reshape((SPANS, KN))
    neighbour_row = place_ends(jax.random.randint(streams_of[6], (SPANS, KN), 0, BLK_DEV), jax.random.fold_in(streams_of[6], 1), 0, BLK_DEV - 1).astype(jnp.int32)
    return dict(queries=queries, out_grad=out_grad, enc_table=enc_table, key_weight=key_weight, value_weight=value_weight, neighbour_owner=neighbour_owner, neighbour_row=neighbour_row)


def attend_span(shifted, gradient, keys, values, score_scale):
    shifted_f = shifted.astype(jnp.float32)
    gradient_f = gradient.astype(jnp.float32)
    keys_f = keys.astype(jnp.float32)
    values_f = values.astype(jnp.float32)
    scores = jnp.einsum('cmhd,ckhd->chmk', shifted_f, keys_f) * score_scale
    weights = jax.nn.softmax(scores, axis=-1)
    rounded = lax.optimization_barrier(weights.astype(jnp.bfloat16)).astype(jnp.float32)
    attended = jnp.einsum('chmk,ckhd->cmhd', rounded, values_f)
    row_delta = jnp.transpose(lax.optimization_barrier(jnp.sum(gradient_f * attended, axis=-1)), (0, 2, 1))
    value_grad = jnp.einsum('chmk,cmhd->ckhd', rounded, gradient_f).astype(jnp.bfloat16)
    product = jnp.einsum('cmhd,ckhd->chmk', gradient_f, values_f)
    score_grad = (weights * (product - row_delta[..., None])).astype(jnp.bfloat16)
    score_grad_f = lax.optimization_barrier(score_grad).astype(jnp.float32)
    query_grad = jnp.einsum('chmk,ckhd->cmhd', score_grad_f, keys_f) * score_scale
    key_grad = (jnp.einsum('chmk,cmhd->ckhd', score_grad_f, shifted_f) * score_scale).astype(jnp.bfloat16)
    return (query_grad, key_grad, value_grad)

def reference(queries, out_grad, enc_table, key_weight, value_weight, neighbour_owner, neighbour_row):
    head_columns = HEADS * DH
    ids = (neighbour_owner * BLK_DEV + neighbour_row).astype(jnp.int32)
    positions = lax.iota(jnp.int32, TOKENS)
    in_sequence = positions % SEQ_LEN <= SEQ_LEN - M
    padding = jnp.zeros((M - 1, head_columns), jnp.bfloat16)
    zero_value = jnp.zeros((), jnp.bfloat16)
    shifted = jnp.where(in_sequence[:, None], jnp.concatenate([queries[M - 1:], padding], 0), zero_value)
    shifted_grad = jnp.where(in_sequence[:, None], jnp.concatenate([out_grad[M - 1:], padding], 0), zero_value)
    joint_weight = jnp.concatenate([key_weight, value_weight], 1)
    score_scale = 1.0 / math.sqrt(DH)

    def one_span(table_grad, inputs):
        span_queries, span_grad, span_ids = inputs
        blocks = jnp.transpose(enc_table[span_ids], (0, 2, 1)).reshape(KN * R, DE)
        projected = jnp.dot(blocks, joint_weight, preferred_element_type=jnp.float32).astype(jnp.bfloat16)
        keys = projected[:, :head_columns].reshape(1, KN * R, HEADS, DH)
        values = projected[:, head_columns:].reshape(1, KN * R, HEADS, DH)
        query_grad, key_grad, value_grad = attend_span(span_queries.reshape(1, M, HEADS, DH), span_grad.reshape(1, M, HEADS, DH), keys, values, score_scale)
        both_grads = jnp.concatenate([key_grad.reshape(KN * R, head_columns), value_grad.reshape(KN * R, head_columns)], 1)
        partial_value = jnp.dot(both_grads, joint_weight.T, preferred_element_type=jnp.float32)
        partial_value = jnp.transpose(partial_value.reshape(KN, R, DE), (0, 2, 1))
        table_grad = table_grad.at[span_ids].add(partial_value)
        return (table_grad, query_grad.reshape(M, head_columns))
    start_grad = jnp.zeros((NBLK, DE, R), jnp.float32)
    table_grad, span_dq = lax.scan(one_span, start_grad, (shifted.reshape(SPANS, M, head_columns), shifted_grad.reshape(SPANS, M, head_columns), ids))
    dq_rounded = span_dq.reshape(TOKENS, head_columns).astype(jnp.bfloat16)
    d_query = jnp.concatenate([padding, dq_rounded[:TOKENS - M + 1]], 0)
    return (d_query, table_grad)
```

```python
import functools
import math

import jax
import jax.numpy as jnp
from jax import lax
from jax.experimental import pallas as pl
from jax.experimental.pallas import tpu as pltpu
from jax.sharding import PartitionSpec as P

M = 64
KN = 2
R = 128
DE = 896
DH = 128
SEQ_LEN = 2048
Z = 4
MESH = pl.DeviceIdType.MESH
F32 = jnp.float32
BF16 = jnp.bfloat16


def dot(a, b):
    return jnp.dot(a, b, preferred_element_type=F32)


def dot_nt(a, b):
    return lax.dot_general(a, b, (((1,), (1,)), ((), ())), preferred_element_type=F32)


def dot_tn(a, b):
    return lax.dot_general(a, b, (((0,), (0,)), ((), ())), preferred_element_type=F32)


def main_kernel(
    nseq, cap, heads,
    own_s, row_s, q_h, g_h, tab_h, kw_h, vw_h,
    dq_o, prev_o, back_o, reqs_o,
    tab, qv, gv, wp, wt, qf, qs, gs, tails,
    req, uos, reqs, reqs_s, uos_s, slot_s,
    send_a, recv_a, gat, kvt, grad_t, dq,
    sib_s, sib_r, own_p, s1_s, s1_r, s2_s, s2_r, res, send_b,
    loc_sem, id_sem, tail_sem, a_sem, f_sem, b_sem, e_sem, dqt_sem,
):
    spans = qs.shape[0]
    uses = spans * KN
    de_e = tab.shape[1]
    cols = heads * DH
    scale = 1.0 / math.sqrt(DH)
    s = lax.axis_index("seq")
    e = lax.axis_index("enc")
    z, core = e // 2, e % 2
    zp, zm, zo = (z + 1) % Z, (z + 3) % Z, (z + 2) % Z
    sib = (s, z * 2 + 1 - core)
    up, down = (s, zp * 2 + core), (s, zm * 2 + core)
    per_seq = SEQ_LEN // (spans * M)
    ring = min(per_seq, nseq)
    base = (s // ring) * ring
    following = (base + (s + 1) % ring, e)
    preceding = (base + (s + ring - 1) % ring, e)

    def remote(src, dst, sem, where):
        return pltpu.make_async_remote_copy(
            src_ref=src, dst_ref=dst, send_sem=sem.at[0], recv_sem=sem.at[1],
            device_id=where, device_id_type=MESH,
        )

    barrier = pltpu.get_barrier_semaphore()

    def greet(i, _):
        pl.semaphore_signal(barrier, inc=1, device_id=((s + i) % nseq, e), device_id_type=MESH)
        return 0

    lax.fori_loop(1, nseq, greet, 0)
    for where in (sib, up, down):
        pl.semaphore_signal(barrier, inc=1, device_id=where, device_id_type=MESH)

    local = [
        pltpu.make_async_copy(tab_h, tab, loc_sem.at[0]),
        pltpu.make_async_copy(q_h, qv, loc_sem.at[1]),
        pltpu.make_async_copy(g_h, gv, loc_sem.at[2]),
        pltpu.make_async_copy(kw_h.at[:, core], wp.at[0, :, :, pl.ds(0, cols)], loc_sem.at[3]),
        pltpu.make_async_copy(vw_h.at[:, core], wp.at[0, :, :, pl.ds(cols, cols)], loc_sem.at[4]),
        pltpu.make_async_copy(kw_h.at[:, 1 - core], wp.at[1, :, :, pl.ds(0, cols)], loc_sem.at[5]),
        pltpu.make_async_copy(vw_h.at[:, 1 - core], wp.at[1, :, :, pl.ds(cols, cols)], loc_sem.at[6]),
    ]
    for c in local:
        c.start()

    lane = lax.broadcasted_iota(jnp.int32, (1, 128), 1)
    lane_owner, lane_k = lane // cap, lane % cap
    count = jnp.zeros((1, 128), jnp.int32)
    rows = jnp.full((1, 128), -1, jnp.int32)
    use_of = jnp.zeros((1, 128), jnp.int32)
    owners = [own_s[u // KN, u % KN] for u in range(uses)]
    for u in range(uses):
        hit = lane_owner == owners[u]
        chosen = hit & (count == lane_k)
        rows = jnp.where(chosen, row_s[u // KN, u % KN], rows)
        use_of = jnp.where(chosen, u, use_of)
        count = count + hit.astype(jnp.int32)
        rank = jnp.int32(0)
        for v in range(u):
            rank = rank + (owners[v] == owners[u]).astype(jnp.int32)
        slot_s[u] = owners[u] * cap + rank
    req[...] = rows
    uos[...] = use_of
    reqs[s] = rows
    uos_copy = pltpu.make_async_copy(uos, uos_s, loc_sem.at[7])
    uos_copy.start()

    pl.semaphore_wait(barrier, nseq - 1 + 3)

    def id_copy(i):
        return remote(req, reqs.at[s], id_sem.at[i], ((s + i) % nseq, e))

    def send_ids(i, _):
        id_copy(i).start()
        return 0

    lax.fori_loop(1, nseq, send_ids, 0)
    q_tail = remote(q_h.at[pl.ds(0, M)], tails.at[0], tail_sem.at[0], preceding)
    g_tail = remote(g_h.at[pl.ds(0, M)], tails.at[1], tail_sem.at[1], preceding)

    def wait_ids(i, _):
        id_copy(i).wait_recv()
        return 0

    lax.fori_loop(1, nseq, wait_ids, 0)
    reqs_copy = pltpu.make_async_copy(reqs, reqs_s, loc_sem.at[8])
    reqs_copy.start()
    reqs_out = pltpu.make_async_copy(reqs, reqs_o, loc_sem.at[9])
    reqs_out.start()
    local[0].wait()
    reqs_copy.wait()

    def a_copy(i):
        peer = (s + i) % nseq
        return remote(send_a.at[peer], recv_a.at[s], a_sem.at[i], (peer, e))

    def send_rows(i, _):
        peer = (s + i) % nseq
        for k in range(cap):
            wanted = jnp.maximum(reqs_s[peer, 0, s * cap + k], 0)
            send_a[peer, k] = tab[wanted]
        a_copy(i).start()
        return 0

    lax.fori_loop(1, nseq, send_rows, 0)
    q_tail.start()
    g_tail.start()
    for k in range(cap):
        recv_a[s, k] = tab[jnp.maximum(reqs_s[s, 0, s * cap + k], 0)]

    for c in local[3:]:
        c.wait()

    def turn(b, _):
        at = pl.ds(pl.multiple_of(b * 128, 128), 128)
        wt[at, :] = wp[:, :, :, at].reshape(DE, 128).T
        return 0

    lax.fori_loop(0, 2 * cols // 128, turn, 0)
    local[1].wait()
    local[2].wait()
    q_tail.wait_recv()
    g_tail.wait_recv()
    inside = jnp.logical_and(s % per_seq != per_seq - 1, s != nseq - 1).astype(F32)
    for index, (source, target) in enumerate(((qv, qs), (gv, gs))):
        qf[pl.ds(0, spans * M), :] = source[...].astype(F32)
        qf[pl.ds(spans * M, M), :] = tails[index].astype(F32) * inside
        for c in range(spans):
            target[c] = qf[pl.ds(c * M + M - 1, M), :].astype(BF16)
    uos_copy.wait()

    def wait_rows(i, _):
        a_copy(i).wait_recv()
        return 0

    lax.fori_loop(1, nseq, wait_rows, 0)

    def f_up(j):
        return remote(gat.at[j, :, 0, z], gat.at[j, :, 0, z], f_sem.at[0, j], up)

    def f_down(j):
        return remote(gat.at[j, :, 0, z], gat.at[j, :, 0, z], f_sem.at[1, j], down)

    def f_half_up(j):
        return remote(gat.at[j, 0, 0, zm], gat.at[j, 0, 0, zm], f_sem.at[2, j], up)

    def f_half_down(j):
        return remote(gat.at[j, 1, 0, zp], gat.at[j, 1, 0, zp], f_sem.at[3, j], down)

    def f_sib(j, which, at):
        return remote(gat.at[j, :, 0, at], gat.at[j, :, 1, at], f_sem.at[4 + which, j], sib)

    def sibs(j):
        return [f_sib(j, 0, z), f_sib(j, 1, zm), f_sib(j, 2, zp), f_sib(j, 3, zo)]

    def b_sib(j):
        return remote(sib_s.at[j], sib_r.at[j], b_sem.at[0, j], sib)

    def b_one(j, d):
        return remote(s1_s.at[j, d], s1_r.at[j, d], b_sem.at[1 + d, j], (up, down)[d])

    def b_two(j, d):
        return remote(s2_s.at[j, d], s2_r.at[j, d], b_sem.at[3 + d, j], (up, down)[d])

    def forward_0(j):
        for t in range(KN):
            slot = slot_s[j * KN + t]
            gat[j, t, 0, z] = recv_a[slot // cap, slot % cap]
        f_up(j).start()
        f_down(j).start()
        f_sib(j, 0, z).start()

    def forward_1(j):
        f_up(j).wait_recv()
        f_half_up(j).start()
        f_sib(j, 1, zm).start()
        f_down(j).wait_recv()
        f_half_down(j).start()
        f_sib(j, 2, zp).start()

    def forward_2(j):
        f_half_up(j).wait_recv()
        f_half_down(j).wait_recv()
        f_sib(j, 3, zo).start()

    def forward_3(j):
        for c in sibs(j):
            c.wait_recv()

    def compute(j):
        blocks = jnp.concatenate([gat[j, t].reshape(DE, R) for t in range(KN)], axis=1)
        kvt[...] = dot(wt[...], blocks).astype(BF16)
        for h in range(heads):
            at = slice(h * DH, (h + 1) * DH)
            at_v = slice(cols + h * DH, cols + (h + 1) * DH)
            query, gradient = qs[j, :, at], gs[j, :, at]
            keys, values = kvt[at, :], kvt[at_v, :]
            scores = dot(query, keys) * scale
            powers = jnp.exp(scores - jnp.max(scores, axis=-1, keepdims=True))
            weights = powers / jnp.sum(powers, axis=-1, keepdims=True)
            rounded = weights.astype(BF16)
            product = dot(gradient, values)
            row_delta = jnp.sum(rounded.astype(F32) * product, axis=-1, keepdims=True)
            score_grad = (weights * (product - row_delta)).astype(BF16)
            dq[j, :, at] = (dot_nt(score_grad, keys) * scale).astype(BF16)
            grad_t[at, :] = (dot_tn(query, score_grad) * scale).astype(BF16)
            grad_t[at_v, :] = dot_tn(gradient, rounded).astype(BF16)
        other = dot(wp[1].reshape(DE // 2, 2 * cols), grad_t[...]).astype(BF16)
        for t in range(KN):
            sib_s[j, t] = other[:, t * R:(t + 1) * R].reshape(Z, de_e, R)
        b_sib(j).start()
        mine = dot(wp[0].reshape(DE // 2, 2 * cols), grad_t[...])
        for t in range(KN):
            own_p[j, t] = mine[:, t * R:(t + 1) * R].reshape(Z, de_e, R)

    def backward_1(j):
        b_sib(j).wait_recv()
        s1_s[j, 0] = (own_p[j, 0, zo] + sib_r[j, 0, zo].astype(F32)).astype(BF16)
        b_one(j, 0).start()
        s1_s[j, 1] = (own_p[j, 1, zo] + sib_r[j, 1, zo].astype(F32)).astype(BF16)
        b_one(j, 1).start()

    def backward_2(j):
        for d, at in ((0, zp), (1, zm)):
            b_one(j, d).wait_recv()
            for t in range(KN):
                term = own_p[j, t, at] + sib_r[j, t, at].astype(F32)
                if t == d:
                    term = term + s1_r[j, d].astype(F32)
                s2_s[j, d, t] = term.astype(BF16)
            b_two(j, d).start()

    def backward_3(j):
        for d in range(2):
            b_two(j, d).wait_recv()
        for t in range(KN):
            term = own_p[j, t, z] + sib_r[j, t, z].astype(F32)
            term = term + s2_r[j, 0, t].astype(F32) + s2_r[j, 1, t].astype(F32)
            res[j * KN + t] = term.astype(BF16)

    stages = (
        (0, forward_0), (1, forward_1), (2, forward_2), (5, backward_2), (6, backward_3),
        (3, forward_3), (3, compute), (4, backward_1),
    )

    def step(i, _):
        for offset, stage in stages:
            j = i - offset

            @pl.when(jnp.logical_and(j >= 0, j < spans))
            def _():
                stage(j)

        return 0

    lax.fori_loop(0, spans + 6, step, 0)

    dq_tail = remote(dq.at[spans - 1], prev_o, dqt_sem, following)
    dq_tail.start()
    dq_out = pltpu.make_async_copy(dq, dq_o, loc_sem.at[10])
    dq_out.start()

    def e_copy(i):
        peer = (s + i) % nseq
        return remote(send_b.at[peer], back_o.at[s], e_sem.at[i], (peer, e))

    def send_terms(i, _):
        peer = (s + i) % nseq
        for k in range(cap):
            send_b[peer, k] = res[uos_s[0, peer * cap + k]]
        e_copy(i).start()
        return 0

    lax.fori_loop(1, nseq, send_terms, 0)
    for k in range(cap):
        send_b[s, k] = res[uos_s[0, s * cap + k]]
    own_back = pltpu.make_async_copy(send_b.at[s], back_o.at[s], loc_sem.at[11])
    own_back.start()

    def drain(j, _):
        for c in [f_up(j), f_down(j), f_half_up(j), f_half_down(j)] + sibs(j):
            c.wait_send()
        for c in (b_sib(j), b_one(j, 0), b_one(j, 1), b_two(j, 0), b_two(j, 1)):
            c.wait_send()
        return 0

    lax.fori_loop(0, spans, drain, 0)

    def drain_peers(i, _):
        id_copy(i).wait_send()
        a_copy(i).wait_send()
        e_copy(i).wait()
        return 0

    lax.fori_loop(1, nseq, drain_peers, 0)
    q_tail.wait_send()
    g_tail.wait_send()
    dq_tail.wait()
    dq_out.wait()
    own_back.wait()
    reqs_out.wait()


def last_kernel(nseq, cap, reqs_s, back, dq, prev, dquery_o, dtable_o, shift):
    s = lax.axis_index("seq")
    rows = dquery_o.shape[0]
    per_seq = SEQ_LEN // rows
    shift[pl.ds(0, M), :] = prev[...].astype(F32) * (s % per_seq != 0).astype(F32)
    shift[pl.ds(M, rows), :] = dq[...].reshape(rows, dq.shape[2]).astype(F32)
    dquery_o[...] = shift[pl.ds(1, rows), :].astype(BF16)
    dtable_o[...] = jnp.zeros_like(dtable_o)

    def add(i, _):
        row = reqs_s[i // cap, 0, s * cap + i % cap]

        @pl.when(row >= 0)
        def _():
            dtable_o[row] += back[i // cap, i % cap].astype(F32)

        return 0

    lax.fori_loop(0, nseq * cap, add, 0)


def local(queries, out_grad, enc_table, key_weight, value_weight, neighbour_owner, neighbour_row):
    nseq = lax.axis_size("seq")
    tok_rows, cols = queries.shape
    heads = cols // DH
    spans = tok_rows // M
    uses = spans * KN
    cap = max(2, uses // nseq)
    blocks, de_e, _ = enc_table.shape
    any_spec = pl.BlockSpec(memory_space=pl.ANY)
    smem = pl.BlockSpec(memory_space=pltpu.SMEM)
    vmem = pl.BlockSpec(memory_space=pltpu.VMEM)
    piece = (de_e, R)
    dma = pltpu.SemaphoreType.DMA
    dq, prev, back, reqs = pl.pallas_call(
        functools.partial(main_kernel, nseq, cap, heads),
        out_shape=(
            jax.ShapeDtypeStruct((spans, M, cols), BF16),
            jax.ShapeDtypeStruct((M, cols), BF16),
            jax.ShapeDtypeStruct((nseq, cap) + piece, BF16),
            jax.ShapeDtypeStruct((nseq, 1, 128), jnp.int32),
        ),
        in_specs=[smem, smem] + [any_spec] * 5,
        out_specs=(any_spec,) * 4,
        scratch_shapes=[
            pltpu.VMEM((blocks,) + piece, BF16),
            pltpu.VMEM((tok_rows, cols), BF16),
            pltpu.VMEM((tok_rows, cols), BF16),
            pltpu.VMEM((2, Z, de_e, 2 * cols), BF16),
            pltpu.VMEM((2 * cols, DE), BF16),
            pltpu.VMEM((tok_rows + M, cols), F32),
            pltpu.VMEM((spans, M, cols), BF16),
            pltpu.VMEM((spans, M, cols), BF16),
            pltpu.VMEM((2, M, cols), BF16),
            pltpu.VMEM((1, 128), jnp.int32),
            pltpu.VMEM((1, 128), jnp.int32),
            pltpu.VMEM((nseq, 1, 128), jnp.int32),
            pltpu.SMEM((nseq, 1, 128), jnp.int32),
            pltpu.SMEM((1, 128), jnp.int32),
            pltpu.SMEM((uses,), jnp.int32),
            pltpu.VMEM((nseq, cap) + piece, BF16),
            pltpu.VMEM((nseq, cap) + piece, BF16),
            pltpu.VMEM((spans, KN, 2, Z) + piece, BF16),
            pltpu.VMEM((2 * cols, KN * R), BF16),
            pltpu.VMEM((2 * cols, KN * R), BF16),
            pltpu.VMEM((spans, M, cols), BF16),
            pltpu.VMEM((spans, KN, Z) + piece, BF16),
            pltpu.VMEM((spans, KN, Z) + piece, BF16),
            pltpu.VMEM((spans, KN, Z) + piece, F32),
            pltpu.VMEM((spans, 2) + piece, BF16),
            pltpu.VMEM((spans, 2) + piece, BF16),
            pltpu.VMEM((spans, 2, KN) + piece, BF16),
            pltpu.VMEM((spans, 2, KN) + piece, BF16),
            pltpu.VMEM((uses,) + piece, BF16),
            pltpu.VMEM((nseq, cap) + piece, BF16),
            dma((12,)),
            dma((nseq, 2)),
            dma((2, 2)),
            dma((nseq, 2)),
            dma((8, spans, 2)),
            dma((5, spans, 2)),
            dma((nseq, 2)),
            dma((2,)),
        ],
        compiler_params=pltpu.CompilerParams(
            collective_id=0, has_side_effects=True, vmem_limit_bytes=56 * 2**20
        ),
    )(
        neighbour_owner, neighbour_row, queries, out_grad, enc_table,
        key_weight.reshape(Z, 2, de_e, cols), value_weight.reshape(Z, 2, de_e, cols),
    )
    return pl.pallas_call(
        functools.partial(last_kernel, nseq, cap),
        out_shape=(
            jax.ShapeDtypeStruct((tok_rows, cols), BF16),
            jax.ShapeDtypeStruct((blocks,) + piece, F32),
        ),
        in_specs=[smem, vmem, vmem, vmem],
        out_specs=(vmem, vmem),
        scratch_shapes=[pltpu.VMEM((tok_rows + M, cols), F32)],
        compiler_params=pltpu.CompilerParams(vmem_limit_bytes=32 * 2**20),
    )(reqs, back, dq, prev)


def solution(mesh):
    in_specs = (
        P("seq", "enc"),
        P("seq", "enc"),
        P("seq", "enc", None),
        P(None, "enc"),
        P(None, "enc"),
        P("seq", None),
        P("seq", None),
    )
    out_specs = (P("seq", "enc"), P("seq", "enc", None))
    return jax.shard_map(local, mesh=mesh, in_specs=in_specs, out_specs=out_specs, check_vma=False)
```

```python
import functools
import math

import jax
import jax.numpy as jnp
from jax import lax
from jax.experimental import pallas as pl
from jax.experimental.pallas import tpu as pltpu
from jax.sharding import PartitionSpec as P

M = 64
KN = 2
R = 128
DE = 896
DH = 128
SEQ_LEN = 2048
Z = 4
MESH = pl.DeviceIdType.MESH
F32 = jnp.float32
BF16 = jnp.bfloat16


def dot(a, b):
    return jnp.dot(a, b, preferred_element_type=F32)


def dot_nt(a, b):
    return lax.dot_general(a, b, (((1,), (1,)), ((), ())), preferred_element_type=F32)


def main_kernel(
    nseq, cap, heads,
    own_h, row_h, q_h, g_h, tab_h, kw_h, vw_h,
    dq_o, prev_o, back_o, reqs_o,
    own_s, row_s, tab, qv, gv, wp, wt, qf, qs, gs, qt, gt, tails,
    req, uos, reqs, reqs_s, uos_s, slot_s,
    send_a, recv_a, gat, kvt, grad_t, dq,
    terms, sib_r, s1_s, s1_r, s2_s, s2_r, res, send_b,
    loc_sem, id_sem, tail_sem, a_sem, f_sem, b_sem, e_sem, dqt_sem,
):
    spans = qs.shape[0]
    uses = spans * KN
    de_e = tab.shape[1]
    cols = heads * DH
    scale = 1.0 / math.sqrt(DH)
    s = lax.axis_index("seq")
    e = lax.axis_index("enc")
    z, core = e // 2, e % 2
    zp, zm, zo = (z + 1) % Z, (z + 3) % Z, (z + 2) % Z
    sib = (s, z * 2 + 1 - core)
    up, down = (s, zp * 2 + core), (s, zm * 2 + core)
    per_seq = SEQ_LEN // (spans * M)
    ring = min(per_seq, nseq)
    base = (s // ring) * ring
    following = (base + (s + 1) % ring, e)
    preceding = (base + (s + ring - 1) % ring, e)

    def remote(src, dst, sem, where):
        return pltpu.make_async_remote_copy(
            src_ref=src, dst_ref=dst, send_sem=sem.at[0], recv_sem=sem.at[1],
            device_id=where, device_id_type=MESH,
        )

    barrier = pltpu.get_barrier_semaphore()

    def greet(i, _):
        pl.semaphore_signal(barrier, inc=1, device_id=((s + i) % nseq, e), device_id_type=MESH)
        return 0

    lax.fori_loop(1, nseq, greet, 0)
    for where in (sib, up, down):
        pl.semaphore_signal(barrier, inc=1, device_id=where, device_id_type=MESH)

    ids_in = [
        pltpu.make_async_copy(own_h, own_s, loc_sem.at[12]),
        pltpu.make_async_copy(row_h, row_s, loc_sem.at[13]),
    ]
    for c in ids_in:
        c.start()
    local = [
        pltpu.make_async_copy(tab_h, tab, loc_sem.at[0]),
        pltpu.make_async_copy(q_h, qv, loc_sem.at[1]),
        pltpu.make_async_copy(g_h, gv, loc_sem.at[2]),
        pltpu.make_async_copy(kw_h.at[:, core], wp.at[0, :, :, pl.ds(0, cols)], loc_sem.at[3]),
        pltpu.make_async_copy(vw_h.at[:, core], wp.at[0, :, :, pl.ds(cols, cols)], loc_sem.at[4]),
        pltpu.make_async_copy(kw_h.at[:, 1 - core], wp.at[1, :, :, pl.ds(0, cols)], loc_sem.at[5]),
        pltpu.make_async_copy(vw_h.at[:, 1 - core], wp.at[1, :, :, pl.ds(cols, cols)], loc_sem.at[6]),
    ]
    for c in local:
        c.start()

    for c in ids_in:
        c.wait()

    lane = lax.broadcasted_iota(jnp.int32, (1, 128), 1)
    lane_owner, lane_k = lane // cap, lane % cap
    count = jnp.zeros((1, 128), jnp.int32)
    rows = jnp.full((1, 128), -1, jnp.int32)
    use_of = jnp.zeros((1, 128), jnp.int32)
    owners = [own_s[u % KN, u // KN] for u in range(uses)]
    for u in range(uses):
        hit = lane_owner == owners[u]
        chosen = hit & (count == lane_k)
        rows = jnp.where(chosen, row_s[u % KN, u // KN], rows)
        use_of = jnp.where(chosen, u, use_of)
        count = count + hit.astype(jnp.int32)
        rank = jnp.int32(0)
        for v in range(u):
            rank = rank + (owners[v] == owners[u]).astype(jnp.int32)
        slot_s[u] = owners[u] * cap + rank
    req[...] = rows
    uos[...] = use_of
    reqs[s] = rows
    uos_copy = pltpu.make_async_copy(uos, uos_s, loc_sem.at[7])
    uos_copy.start()

    pl.semaphore_wait(barrier, nseq - 1 + 3)

    def id_copy(i):
        return remote(req, reqs.at[s], id_sem.at[i], ((s + i) % nseq, e))

    def send_ids(i, _):
        id_copy(i).start()
        return 0

    lax.fori_loop(1, nseq, send_ids, 0)
    q_tail = remote(q_h.at[pl.ds(0, M)], tails.at[0], tail_sem.at[0], preceding)
    g_tail = remote(g_h.at[pl.ds(0, M)], tails.at[1], tail_sem.at[1], preceding)

    q_tail.start()
    g_tail.start()

    for c in local[3:]:
        c.wait()

    def turn(b, _):
        at = pl.ds(pl.multiple_of(b * 128, 128), 128)
        wt[at, :] = wp[:, :, :, at].reshape(DE, 128).T
        return 0

    lax.fori_loop(0, 2 * cols // 128, turn, 0)

    def shift(index, c):
        moved = qf[index, pl.ds(c * M + M - 1, M), :].astype(BF16)
        (qs, gs)[index][c] = moved
        (qt, gt)[index][c] = moved.T

    for index, source in enumerate((qv, gv)):
        local[1 + index].wait()
        qf[index, pl.ds(0, spans * M), :] = source[...].astype(F32)
        for c in range(spans - 1):
            shift(index, c)

    def wait_ids(i, _):
        id_copy(i).wait_recv()
        return 0

    lax.fori_loop(1, nseq, wait_ids, 0)
    reqs_copy = pltpu.make_async_copy(reqs, reqs_s, loc_sem.at[8])
    reqs_copy.start()
    reqs_out = pltpu.make_async_copy(reqs, reqs_o, loc_sem.at[9])
    reqs_out.start()
    local[0].wait()
    reqs_copy.wait()

    def a_copy(i):
        peer = (s + i) % nseq
        return remote(send_a.at[peer], recv_a.at[s], a_sem.at[i], (peer, e))

    def send_rows(i, _):
        peer = (s + i) % nseq
        for k in range(cap):
            wanted = jnp.maximum(reqs_s[peer, 0, s * cap + k], 0)
            send_a[peer, k] = tab[wanted]
        a_copy(i).start()
        return 0

    lax.fori_loop(1, nseq, send_rows, 0)
    for k in range(cap):
        recv_a[s, k] = tab[jnp.maximum(reqs_s[s, 0, s * cap + k], 0)]

    q_tail.wait_recv()
    g_tail.wait_recv()
    inside = jnp.logical_and(s % per_seq != per_seq - 1, s != nseq - 1).astype(F32)
    for index in range(2):
        qf[index, pl.ds(spans * M, M), :] = tails[index].astype(F32) * inside
        shift(index, spans - 1)
    uos_copy.wait()

    def wait_rows(i, _):
        a_copy(i).wait_recv()
        return 0

    lax.fori_loop(1, nseq, wait_rows, 0)

    def f_up(j):
        return remote(gat.at[j, :, 0, z], gat.at[j, :, 0, z], f_sem.at[0, j], up)

    def f_down(j):
        return remote(gat.at[j, :, 0, z], gat.at[j, :, 0, z], f_sem.at[1, j], down)

    def f_half_up(j):
        return remote(gat.at[j, 0, 0, zm], gat.at[j, 0, 0, zm], f_sem.at[2, j], up)

    def f_half_down(j):
        return remote(gat.at[j, 1, 0, zp], gat.at[j, 1, 0, zp], f_sem.at[3, j], down)

    def f_sib(j, which, at):
        return remote(gat.at[j, :, 0, at], gat.at[j, :, 1, at], f_sem.at[4 + which, j], sib)

    def sibs(j):
        return [f_sib(j, 0, z), f_sib(j, 1, zm), f_sib(j, 2, zp), f_sib(j, 3, zo)]

    def b_sib(j):
        return remote(terms.at[1, j], sib_r.at[j], b_sem.at[0, j], sib)

    def b_one(j, d):
        return remote(s1_s.at[j, d], s1_r.at[j, d], b_sem.at[1 + d, j], (up, down)[d])

    def b_two(j, d):
        return remote(s2_s.at[j, d], s2_r.at[j, d], b_sem.at[3 + d, j], (up, down)[d])

    def forward_0(j):
        for t in range(KN):
            slot = slot_s[j * KN + t]
            gat[j, t, 0, z] = recv_a[slot // cap, slot % cap]
        f_up(j).start()
        f_down(j).start()
        f_sib(j, 0, z).start()

    def forward_1(j):
        f_up(j).wait_recv()
        f_half_up(j).start()
        f_sib(j, 1, zm).start()
        f_down(j).wait_recv()
        f_half_down(j).start()
        f_sib(j, 2, zp).start()

    def forward_2(j):
        f_half_up(j).wait_recv()
        f_half_down(j).wait_recv()
        f_sib(j, 3, zo).start()

    def forward_3(j):
        for c in sibs(j):
            c.wait_recv()

    def project(j):
        half = cols

        def some(b, _):
            at = pl.ds(pl.multiple_of(b * half, half), half)
            blocks = jnp.concatenate([gat[j, t].reshape(DE, R) for t in range(KN)], axis=1)
            kvt[at, :] = dot(wt[at, :], blocks).astype(BF16)
            return 0

        lax.fori_loop(0, 2, some, 0)

    def attend(j):
        hs = range(heads)
        at = [slice(h * DH, (h + 1) * DH) for h in hs]
        at_v = [slice(cols + h * DH, cols + (h + 1) * DH) for h in hs]
        scores = [dot(qs[j, :, at[h]], kvt[at[h], :]) * (scale * math.log2(math.e)) for h in hs]
        product = [dot(gs[j, :, at[h]], kvt[at_v[h], :]) for h in hs]
        powers = [jnp.exp2(x - jnp.max(x, axis=-1, keepdims=True)) for x in scores]
        weights = [x * (1.0 / jnp.sum(x, axis=-1, keepdims=True)) for x in powers]
        rounded = [x.astype(BF16) for x in weights]
        row_delta = [
            jnp.sum(x.astype(F32) * y, axis=-1, keepdims=True) for x, y in zip(rounded, product)
        ]
        score_grad = [(x * (y - d)).astype(BF16) for x, y, d in zip(weights, product, row_delta)]
        for h in hs:
            grad_t[at_v[h], :] = dot(gt[j, at[h], :], rounded[h]).astype(BF16)
        for h in hs:
            dq[j, :, at[h]] = (dot_nt(score_grad[h], kvt[at[h], :]) * scale).astype(BF16)
            grad_t[at[h], :] = (dot(qt[j, at[h], :], score_grad[h]) * scale).astype(BF16)
        for side in (1, 0):
            term = dot(wp[side].reshape(DE // 2, 2 * cols), grad_t[...]).astype(BF16)
            for t in range(KN):
                terms[side, j, t] = term[:, t * R:(t + 1) * R].reshape(Z, de_e, R)
            if side == 1:
                b_sib(j).start()

    def both(j, t, at):
        return terms[0, j, t, at].astype(F32) + sib_r[j, t, at].astype(F32)

    def backward_1(j):
        b_sib(j).wait_recv()
        s1_s[j, 0] = both(j, 0, zo).astype(BF16)
        b_one(j, 0).start()
        s1_s[j, 1] = both(j, 1, zo).astype(BF16)
        b_one(j, 1).start()

    def backward_2(j):
        for d, at in ((0, zp), (1, zm)):
            b_one(j, d).wait_recv()
            for t in range(KN):
                term = both(j, t, at)
                if t == d:
                    term = term + s1_r[j, d].astype(F32)
                s2_s[j, d, t] = term.astype(BF16)
            b_two(j, d).start()

    def backward_3(j):
        for d in range(2):
            b_two(j, d).wait_recv()
        for t in range(KN):
            term = both(j, t, z) + s2_r[j, 0, t].astype(F32) + s2_r[j, 1, t].astype(F32)
            res[j * KN + t] = term.astype(BF16)

    stages = (
        (0, forward_0), (1, forward_1), (2, forward_2), (3, forward_3), (3, project),
        (4, backward_1), (5, backward_2), (6, backward_3), (3, attend),
    )

    def step(i, _):
        for offset, stage in stages:
            j = i - offset

            @pl.when(jnp.logical_and(j >= 0, j < spans))
            def _():
                stage(j)

        return 0

    lax.fori_loop(0, spans + 6, step, 0)

    dq_tail = remote(dq.at[spans - 1], prev_o, dqt_sem, following)
    dq_tail.start()
    dq_out = pltpu.make_async_copy(dq, dq_o, loc_sem.at[10])
    dq_out.start()

    def e_copy(i):
        peer = (s + i) % nseq
        return remote(send_b.at[peer], back_o.at[s], e_sem.at[i], (peer, e))

    def send_terms(i, _):
        peer = (s + i) % nseq
        for k in range(cap):
            send_b[peer, k] = res[uos_s[0, peer * cap + k]]
        e_copy(i).start()
        return 0

    lax.fori_loop(1, nseq, send_terms, 0)
    for k in range(cap):
        send_b[s, k] = res[uos_s[0, s * cap + k]]
    own_back = pltpu.make_async_copy(send_b.at[s], back_o.at[s], loc_sem.at[11])
    own_back.start()

    def drain(j, _):
        for c in [f_up(j), f_down(j), f_half_up(j), f_half_down(j)] + sibs(j):
            c.wait_send()
        for c in (b_sib(j), b_one(j, 0), b_one(j, 1), b_two(j, 0), b_two(j, 1)):
            c.wait_send()
        return 0

    lax.fori_loop(0, spans, drain, 0)

    def drain_peers(i, _):
        id_copy(i).wait_send()
        a_copy(i).wait_send()
        e_copy(i).wait()
        return 0

    lax.fori_loop(1, nseq, drain_peers, 0)
    q_tail.wait_send()
    g_tail.wait_send()
    dq_tail.wait()
    dq_out.wait()
    own_back.wait()
    reqs_out.wait()


def last_kernel(
    nseq, cap, reqs_h, back_h, dq_h, prev_h, dquery_o, dtable_o,
    reqs_s, back, dq, prev, shift, moved, total, sem,
):
    ins = [
        pltpu.make_async_copy(reqs_h, reqs_s, sem.at[0]),
        pltpu.make_async_copy(dq_h, dq, sem.at[1]),
        pltpu.make_async_copy(prev_h, prev, sem.at[2]),
        pltpu.make_async_copy(back_h, back, sem.at[3]),
    ]
    for c in ins:
        c.start()
    total[...] = jnp.zeros_like(total)
    s = lax.axis_index("seq")
    rows = dquery_o.shape[0]
    per_seq = SEQ_LEN // rows
    for c in ins:
        c.wait()

    def add(i, _):
        row = reqs_s[i // cap, 0, s * cap + i % cap]

        @pl.when(row >= 0)
        def _():
            total[row] += back[i // cap, i % cap].astype(F32)

        return 0

    lax.fori_loop(0, nseq * cap, add, 0)
    table_out = pltpu.make_async_copy(total, dtable_o, sem.at[4])
    table_out.start()
    shift[pl.ds(0, M), :] = prev[...].astype(F32) * (s % per_seq != 0).astype(F32)
    shift[pl.ds(M, rows), :] = dq[...].reshape(rows, dq.shape[2]).astype(F32)
    moved[...] = shift[pl.ds(1, rows), :].astype(BF16)
    query_out = pltpu.make_async_copy(moved, dquery_o, sem.at[5])
    query_out.start()
    table_out.wait()
    query_out.wait()


def local(queries, out_grad, enc_table, key_weight, value_weight, neighbour_owner, neighbour_row):
    nseq = lax.axis_size("seq")
    tok_rows, cols = queries.shape
    heads = cols // DH
    spans = tok_rows // M
    uses = spans * KN
    cap = max(2, uses // nseq)
    blocks, de_e, _ = enc_table.shape
    any_spec = pl.BlockSpec(memory_space=pl.ANY)
    piece = (de_e, R)
    dma = pltpu.SemaphoreType.DMA
    dq, prev, back, reqs = pl.pallas_call(
        functools.partial(main_kernel, nseq, cap, heads),
        out_shape=(
            jax.ShapeDtypeStruct((spans, M, cols), BF16),
            jax.ShapeDtypeStruct((M, cols), BF16),
            jax.ShapeDtypeStruct((nseq, cap) + piece, BF16),
            jax.ShapeDtypeStruct((nseq, 1, 128), jnp.int32),
        ),
        in_specs=[any_spec] * 7,
        out_specs=(any_spec,) * 4,
        scratch_shapes=[
            pltpu.SMEM((KN, spans), jnp.int32),
            pltpu.SMEM((KN, spans), jnp.int32),
            pltpu.VMEM((blocks,) + piece, BF16),
            pltpu.VMEM((tok_rows, cols), BF16),
            pltpu.VMEM((tok_rows, cols), BF16),
            pltpu.VMEM((2, Z, de_e, 2 * cols), BF16),
            pltpu.VMEM((2 * cols, DE), BF16),
            pltpu.VMEM((2, tok_rows + M, cols), F32),
            pltpu.VMEM((spans, M, cols), BF16),
            pltpu.VMEM((spans, M, cols), BF16),
            pltpu.VMEM((spans, cols, M), BF16),
            pltpu.VMEM((spans, cols, M), BF16),
            pltpu.VMEM((2, M, cols), BF16),
            pltpu.VMEM((1, 128), jnp.int32),
            pltpu.VMEM((1, 128), jnp.int32),
            pltpu.VMEM((nseq, 1, 128), jnp.int32),
            pltpu.SMEM((nseq, 1, 128), jnp.int32),
            pltpu.SMEM((1, 128), jnp.int32),
            pltpu.SMEM((uses,), jnp.int32),
            pltpu.VMEM((nseq, cap) + piece, BF16),
            pltpu.VMEM((nseq, cap) + piece, BF16),
            pltpu.VMEM((spans, KN, 2, Z) + piece, BF16),
            pltpu.VMEM((2 * cols, KN * R), BF16),
            pltpu.VMEM((2 * cols, KN * R), BF16),
            pltpu.VMEM((spans, M, cols), BF16),
            pltpu.VMEM((2, spans, KN, Z) + piece, BF16),
            pltpu.VMEM((spans, KN, Z) + piece, BF16),
            pltpu.VMEM((spans, 2) + piece, BF16),
            pltpu.VMEM((spans, 2) + piece, BF16),
            pltpu.VMEM((spans, 2, KN) + piece, BF16),
            pltpu.VMEM((spans, 2, KN) + piece, BF16),
            pltpu.VMEM((uses,) + piece, BF16),
            pltpu.VMEM((nseq, cap) + piece, BF16),
            dma((14,)),
            dma((nseq, 2)),
            dma((2, 2)),
            dma((nseq, 2)),
            dma((8, spans, 2)),
            dma((5, spans, 2)),
            dma((nseq, 2)),
            dma((2,)),
        ],
        compiler_params=pltpu.CompilerParams(
            collective_id=0, has_side_effects=True, vmem_limit_bytes=56 * 2**20
        ),
    )(
        neighbour_owner.T, neighbour_row.T, queries, out_grad, enc_table,
        key_weight.reshape(Z, 2, de_e, cols), value_weight.reshape(Z, 2, de_e, cols),
    )
    return pl.pallas_call(
        functools.partial(last_kernel, nseq, cap),
        out_shape=(
            jax.ShapeDtypeStruct((tok_rows, cols), BF16),
            jax.ShapeDtypeStruct((blocks,) + piece, F32),
        ),
        in_specs=[any_spec] * 4,
        out_specs=(any_spec,) * 2,
        scratch_shapes=[
            pltpu.SMEM((nseq, 1, 128), jnp.int32),
            pltpu.VMEM((nseq, cap) + piece, BF16),
            pltpu.VMEM((spans, M, cols), BF16),
            pltpu.VMEM((M, cols), BF16),
            pltpu.VMEM((tok_rows + M, cols), F32),
            pltpu.VMEM((tok_rows, cols), BF16),
            pltpu.VMEM((blocks,) + piece, F32),
            dma((6,)),
        ],
        compiler_params=pltpu.CompilerParams(vmem_limit_bytes=60 * 2**20),
    )(reqs, back, dq, prev)


def solution(mesh):
    in_specs = (
        P("seq", "enc"),
        P("seq", "enc"),
        P("seq", "enc", None),
        P(None, "enc"),
        P(None, "enc"),
        P("seq", None),
        P("seq", None),
    )
    out_specs = (P("seq", "enc"), P("seq", "enc", None))
    return jax.shard_map(local, mesh=mesh, in_specs=in_specs, out_specs=out_specs, check_vma=False)
```

```python
import functools
import math

import jax
import jax.numpy as jnp
from jax import lax
from jax.experimental import pallas as pl
from jax.experimental.pallas import tpu as pltpu
from jax.sharding import PartitionSpec as P

M = 64
KN = 2
R = 128
DE = 896
DH = 128
SEQ_LEN = 2048
Z = 4
MESH = pl.DeviceIdType.MESH
F32 = jnp.float32
BF16 = jnp.bfloat16


def dot(a, b):
    return jnp.dot(a, b, preferred_element_type=F32)


def dot_nt(a, b):
    return lax.dot_general(a, b, (((1,), (1,)), ((), ())), preferred_element_type=F32)


def main_kernel(
    nseq, cap, heads,
    own_h, row_h, q_h, g_h, tab_h, kw_h, vw_h,
    dq_o, prev_o, back_o, reqs_o,
    own_s, row_s, tab, qv, gv, wp, wt, qf, qs, gs, qt, gt, tails,
    req, uos, reqs, reqs_s, uos_s, slot_s,
    send_a, recv_a, gat, kvt, grad_t, dq,
    terms, sib_r, s1_s, s1_r, s2_s, s2_r, res, send_b,
    loc_sem, id_sem, tail_sem, a_sem, f_sem, b_sem, e_sem, dqt_sem,
):
    spans = qs.shape[0]
    uses = spans * KN
    de_e = tab.shape[1]
    cols = heads * DH
    scale = 1.0 / math.sqrt(DH)
    s = lax.axis_index("seq")
    e = lax.axis_index("enc")
    z, core = e // 2, e % 2
    zp, zm, zo = (z + 1) % Z, (z + 3) % Z, (z + 2) % Z
    sib = (s, z * 2 + 1 - core)
    up, down = (s, zp * 2 + core), (s, zm * 2 + core)
    per_seq = SEQ_LEN // (spans * M)
    ring = min(per_seq, nseq)
    base = (s // ring) * ring
    following = (base + (s + 1) % ring, e)
    preceding = (base + (s + ring - 1) % ring, e)

    def remote(src, dst, sem, where):
        return pltpu.make_async_remote_copy(
            src_ref=src, dst_ref=dst, send_sem=sem.at[0], recv_sem=sem.at[1],
            device_id=where, device_id_type=MESH,
        )

    barrier = pltpu.get_barrier_semaphore()

    def greet(i, _):
        pl.semaphore_signal(barrier, inc=1, device_id=((s + i) % nseq, e), device_id_type=MESH)
        return 0

    lax.fori_loop(1, nseq, greet, 0)
    for where in (sib, up, down):
        pl.semaphore_signal(barrier, inc=1, device_id=where, device_id_type=MESH)

    ids_in = [
        pltpu.make_async_copy(own_h, own_s, loc_sem.at[12]),
        pltpu.make_async_copy(row_h, row_s, loc_sem.at[13]),
    ]
    for c in ids_in:
        c.start()
    local = [
        pltpu.make_async_copy(tab_h, tab, loc_sem.at[0]),
        pltpu.make_async_copy(q_h, qv, loc_sem.at[1]),
        pltpu.make_async_copy(g_h, gv, loc_sem.at[2]),
        pltpu.make_async_copy(kw_h.at[:, core], wp.at[0, :, :, pl.ds(0, cols)], loc_sem.at[3]),
        pltpu.make_async_copy(vw_h.at[:, core], wp.at[0, :, :, pl.ds(cols, cols)], loc_sem.at[4]),
        pltpu.make_async_copy(kw_h.at[:, 1 - core], wp.at[1, :, :, pl.ds(0, cols)], loc_sem.at[5]),
        pltpu.make_async_copy(vw_h.at[:, 1 - core], wp.at[1, :, :, pl.ds(cols, cols)], loc_sem.at[6]),
    ]
    for c in local:
        c.start()

    for c in ids_in:
        c.wait()

    lane = lax.broadcasted_iota(jnp.int32, (1, 128), 1)
    lane_owner, lane_k = lane // cap, lane % cap
    count = jnp.zeros((1, 128), jnp.int32)
    rows = jnp.full((1, 128), -1, jnp.int32)
    use_of = jnp.zeros((1, 128), jnp.int32)
    owners = [own_s[u % KN, u // KN] for u in range(uses)]
    for u in range(uses):
        hit = lane_owner == owners[u]
        chosen = hit & (count == lane_k)
        rows = jnp.where(chosen, row_s[u % KN, u // KN], rows)
        use_of = jnp.where(chosen, u, use_of)
        count = count + hit.astype(jnp.int32)
        rank = jnp.int32(0)
        for v in range(u):
            rank = rank + (owners[v] == owners[u]).astype(jnp.int32)
        slot_s[u] = owners[u] * cap + rank
    req[...] = rows
    uos[...] = use_of
    reqs[s] = rows
    uos_copy = pltpu.make_async_copy(uos, uos_s, loc_sem.at[7])
    uos_copy.start()

    pl.semaphore_wait(barrier, nseq - 1 + 3)

    def id_copy(i):
        return remote(req, reqs.at[s], id_sem.at[i], ((s + i) % nseq, e))

    def send_ids(i, _):
        id_copy(i).start()
        return 0

    lax.fori_loop(1, nseq, send_ids, 0)
    q_tail = remote(q_h.at[pl.ds(0, M)], tails.at[0], tail_sem.at[0], preceding)
    g_tail = remote(g_h.at[pl.ds(0, M)], tails.at[1], tail_sem.at[1], preceding)

    q_tail.start()
    g_tail.start()

    for c in local[3:]:
        c.wait()

    def turn(b, _):
        at = pl.ds(pl.multiple_of(b * 128, 128), 128)
        wt[at, :] = wp[:, :, :, at].reshape(DE, 128).T
        return 0

    lax.fori_loop(0, 2 * cols // 128, turn, 0)

    def shift(index, c):
        moved = qf[index, pl.ds(c * M + M - 1, M), :].astype(BF16)
        (qs, gs)[index][c] = moved
        (qt, gt)[index][c] = moved.T

    for index, source in enumerate((qv, gv)):
        local[1 + index].wait()
        qf[index, pl.ds(0, spans * M), :] = source[...].astype(F32)
        for c in range(spans - 1):
            shift(index, c)

    def wait_ids(i, _):
        id_copy(i).wait_recv()
        return 0

    lax.fori_loop(1, nseq, wait_ids, 0)
    reqs_copy = pltpu.make_async_copy(reqs, reqs_s, loc_sem.at[8])
    reqs_copy.start()
    reqs_out = pltpu.make_async_copy(reqs, reqs_o, loc_sem.at[9])
    reqs_out.start()
    local[0].wait()
    reqs_copy.wait()

    def a_copy(i):
        peer = (s + i) % nseq
        return remote(send_a.at[peer], recv_a.at[s], a_sem.at[i], (peer, e))

    def send_rows(i, _):
        peer = (s + i) % nseq
        for k in range(cap):
            wanted = jnp.maximum(reqs_s[peer, 0, s * cap + k], 0)
            send_a[peer, k] = tab[wanted]
        a_copy(i).start()
        return 0

    lax.fori_loop(1, nseq, send_rows, 0)
    for k in range(cap):
        recv_a[s, k] = tab[jnp.maximum(reqs_s[s, 0, s * cap + k], 0)]

    q_tail.wait_recv()
    g_tail.wait_recv()
    inside = jnp.logical_and(s % per_seq != per_seq - 1, s != nseq - 1).astype(F32)
    for index in range(2):
        qf[index, pl.ds(spans * M, M), :] = tails[index].astype(F32) * inside
        shift(index, spans - 1)
    uos_copy.wait()

    def wait_rows(i, _):
        a_copy(i).wait_recv()
        return 0

    lax.fori_loop(1, nseq, wait_rows, 0)

    def f_up(j):
        return remote(gat.at[j, :, 0, z], gat.at[j, :, 0, z], f_sem.at[0, j], up)

    def f_down(j):
        return remote(gat.at[j, :, 0, z], gat.at[j, :, 0, z], f_sem.at[1, j], down)

    def f_half_up(j):
        return remote(gat.at[j, 0, 0, zm], gat.at[j, 0, 0, zm], f_sem.at[2, j], up)

    def f_half_down(j):
        return remote(gat.at[j, 1, 0, zp], gat.at[j, 1, 0, zp], f_sem.at[3, j], down)

    def f_sib(j):
        return remote(gat.at[j, :, 0], gat.at[j, :, 1], f_sem.at[4, j], sib)

    def sibs(j):
        return [f_sib(j)]

    def b_sib(j):
        return remote(terms.at[1, j], sib_r.at[j], b_sem.at[0, j], sib)

    def b_one(j, d):
        return remote(s1_s.at[j, d], s1_r.at[j, d], b_sem.at[1 + d, j], (up, down)[d])

    def b_two(j, d):
        return remote(s2_s.at[j, d], s2_r.at[j, d], b_sem.at[3 + d, j], (up, down)[d])

    def forward_0(j):
        for t in range(KN):
            slot = slot_s[j * KN + t]
            gat[j, t, 0, z] = recv_a[slot // cap, slot % cap]
        f_up(j).start()
        f_down(j).start()

    def forward_1(j):
        f_up(j).wait_recv()
        f_half_up(j).start()
        f_down(j).wait_recv()
        f_half_down(j).start()

    def forward_2(j):
        f_half_up(j).wait_recv()
        f_half_down(j).wait_recv()
        f_sib(j).start()

    def forward_3(j):
        for c in sibs(j):
            c.wait_recv()

    def project(j):
        half = cols

        def some(b, _):
            at = pl.ds(pl.multiple_of(b * half, half), half)
            blocks = jnp.concatenate([gat[j, t].reshape(DE, R) for t in range(KN)], axis=1)
            kvt[at, :] = dot(wt[at, :], blocks).astype(BF16)
            return 0

        lax.fori_loop(0, 2, some, 0)

    def attend(j):
        hs = range(heads)
        at = [slice(h * DH, (h + 1) * DH) for h in hs]
        at_v = [slice(cols + h * DH, cols + (h + 1) * DH) for h in hs]
        scores = [dot(qs[j, :, at[h]], kvt[at[h], :]) * (scale * math.log2(math.e)) for h in hs]
        product = [dot(gs[j, :, at[h]], kvt[at_v[h], :]) for h in hs]
        powers = [jnp.exp2(x - jnp.max(x, axis=-1, keepdims=True)) for x in scores]
        weights = [x * (1.0 / jnp.sum(x, axis=-1, keepdims=True)) for x in powers]
        rounded = [x.astype(BF16) for x in weights]
        row_delta = [
            jnp.sum(x.astype(F32) * y, axis=-1, keepdims=True) for x, y in zip(rounded, product)
        ]
        score_grad = [(x * (y - d)).astype(BF16) for x, y, d in zip(weights, product, row_delta)]
        for h in hs:
            grad_t[at_v[h], :] = dot(gt[j, at[h], :], rounded[h]).astype(BF16)
        for h in hs:
            dq[j, :, at[h]] = (dot_nt(score_grad[h], kvt[at[h], :]) * scale).astype(BF16)
            grad_t[at[h], :] = (dot(qt[j, at[h], :], score_grad[h]) * scale).astype(BF16)
        for side in (1, 0):
            term = dot(wp[side].reshape(DE // 2, 2 * cols), grad_t[...]).astype(BF16)
            for t in range(KN):
                terms[side, j, t] = term[:, t * R:(t + 1) * R].reshape(Z, de_e, R)
            if side == 1:
                b_sib(j).start()

    def both(j, t, at):
        return terms[0, j, t, at].astype(F32) + sib_r[j, t, at].astype(F32)

    def backward_1(j):
        b_sib(j).wait_recv()
        s1_s[j, 0] = both(j, 0, zo).astype(BF16)
        b_one(j, 0).start()
        s1_s[j, 1] = both(j, 1, zo).astype(BF16)
        b_one(j, 1).start()

    def backward_2(j):
        for d, at in ((0, zp), (1, zm)):
            b_one(j, d).wait_recv()
            for t in range(KN):
                term = both(j, t, at)
                if t == d:
                    term = term + s1_r[j, d].astype(F32)
                s2_s[j, d, t] = term.astype(BF16)
            b_two(j, d).start()

    def backward_3(j):
        for d in range(2):
            b_two(j, d).wait_recv()
        for t in range(KN):
            term = both(j, t, z) + s2_r[j, 0, t].astype(F32) + s2_r[j, 1, t].astype(F32)
            res[j * KN + t] = term.astype(BF16)

    stages = ((0, forward_0), (4, forward_2), (2, forward_1), (5, forward_3), (5, project), (10, backward_3), (8, backward_2), (6, backward_1), (5, attend))

    def step(i, _):
        for offset, stage in stages:
            j = i - offset

            @pl.when(jnp.logical_and(j >= 0, j < spans))
            def _():
                stage(j)

        return 0

    lax.fori_loop(0, spans + 10, step, 0)

    dq_tail = remote(dq.at[spans - 1], prev_o, dqt_sem, following)
    dq_tail.start()
    dq_out = pltpu.make_async_copy(dq, dq_o, loc_sem.at[10])
    dq_out.start()

    def e_copy(i):
        peer = (s + i) % nseq
        return remote(send_b.at[peer], back_o.at[s], e_sem.at[i], (peer, e))

    def send_terms(i, _):
        peer = (s + i) % nseq
        for k in range(cap):
            send_b[peer, k] = res[uos_s[0, peer * cap + k]]
        e_copy(i).start()
        return 0

    lax.fori_loop(1, nseq, send_terms, 0)
    for k in range(cap):
        send_b[s, k] = res[uos_s[0, s * cap + k]]
    own_back = pltpu.make_async_copy(send_b.at[s], back_o.at[s], loc_sem.at[11])
    own_back.start()

    def drain(j, _):
        for c in [f_up(j), f_down(j), f_half_up(j), f_half_down(j)] + sibs(j):
            c.wait_send()
        for c in (b_sib(j), b_one(j, 0), b_one(j, 1), b_two(j, 0), b_two(j, 1)):
            c.wait_send()
        return 0

    lax.fori_loop(0, spans, drain, 0)

    def drain_peers(i, _):
        id_copy(i).wait_send()
        a_copy(i).wait_send()
        e_copy(i).wait()
        return 0

    lax.fori_loop(1, nseq, drain_peers, 0)
    q_tail.wait_send()
    g_tail.wait_send()
    dq_tail.wait()
    dq_out.wait()
    own_back.wait()
    reqs_out.wait()


def last_kernel(
    nseq, cap, reqs_h, back_h, dq_h, prev_h, dquery_o, dtable_o,
    reqs_s, back, dq, prev, shift, moved, total, sem,
):
    ins = [
        pltpu.make_async_copy(reqs_h, reqs_s, sem.at[0]),
        pltpu.make_async_copy(dq_h, dq, sem.at[1]),
        pltpu.make_async_copy(prev_h, prev, sem.at[2]),
        pltpu.make_async_copy(back_h, back, sem.at[3]),
    ]
    for c in ins:
        c.start()
    total[...] = jnp.zeros_like(total)
    s = lax.axis_index("seq")
    rows = dquery_o.shape[0]
    per_seq = SEQ_LEN // rows
    for c in ins:
        c.wait()

    def add(i, _):
        row = reqs_s[i // cap, 0, s * cap + i % cap]

        @pl.when(row >= 0)
        def _():
            total[row] += back[i // cap, i % cap].astype(F32)

        return 0

    lax.fori_loop(0, nseq * cap, add, 0)
    table_out = pltpu.make_async_copy(total, dtable_o, sem.at[4])
    table_out.start()
    shift[pl.ds(0, M), :] = prev[...].astype(F32) * (s % per_seq != 0).astype(F32)
    shift[pl.ds(M, rows), :] = dq[...].reshape(rows, dq.shape[2]).astype(F32)
    moved[...] = shift[pl.ds(1, rows), :].astype(BF16)
    query_out = pltpu.make_async_copy(moved, dquery_o, sem.at[5])
    query_out.start()
    table_out.wait()
    query_out.wait()


def local(queries, out_grad, enc_table, key_weight, value_weight, neighbour_owner, neighbour_row):
    nseq = lax.axis_size("seq")
    tok_rows, cols = queries.shape
    heads = cols // DH
    spans = tok_rows // M
    uses = spans * KN
    cap = max(2, uses // nseq)
    blocks, de_e, _ = enc_table.shape
    any_spec = pl.BlockSpec(memory_space=pl.ANY)
    piece = (de_e, R)
    dma = pltpu.SemaphoreType.DMA
    dq, prev, back, reqs = pl.pallas_call(
        functools.partial(main_kernel, nseq, cap, heads),
        out_shape=(
            jax.ShapeDtypeStruct((spans, M, cols), BF16),
            jax.ShapeDtypeStruct((M, cols), BF16),
            jax.ShapeDtypeStruct((nseq, cap) + piece, BF16),
            jax.ShapeDtypeStruct((nseq, 1, 128), jnp.int32),
        ),
        in_specs=[any_spec] * 7,
        out_specs=(any_spec,) * 4,
        scratch_shapes=[
            pltpu.SMEM((KN, spans), jnp.int32),
            pltpu.SMEM((KN, spans), jnp.int32),
            pltpu.VMEM((blocks,) + piece, BF16),
            pltpu.VMEM((tok_rows, cols), BF16),
            pltpu.VMEM((tok_rows, cols), BF16),
            pltpu.VMEM((2, Z, de_e, 2 * cols), BF16),
            pltpu.VMEM((2 * cols, DE), BF16),
            pltpu.VMEM((2, tok_rows + M, cols), F32),
            pltpu.VMEM((spans, M, cols), BF16),
            pltpu.VMEM((spans, M, cols), BF16),
            pltpu.VMEM((spans, cols, M), BF16),
            pltpu.VMEM((spans, cols, M), BF16),
            pltpu.VMEM((2, M, cols), BF16),
            pltpu.VMEM((1, 128), jnp.int32),
            pltpu.VMEM((1, 128), jnp.int32),
            pltpu.VMEM((nseq, 1, 128), jnp.int32),
            pltpu.SMEM((nseq, 1, 128), jnp.int32),
            pltpu.SMEM((1, 128), jnp.int32),
            pltpu.SMEM((uses,), jnp.int32),
            pltpu.VMEM((nseq, cap) + piece, BF16),
            pltpu.VMEM((nseq, cap) + piece, BF16),
            pltpu.VMEM((spans, KN, 2, Z) + piece, BF16),
            pltpu.VMEM((2 * cols, KN * R), BF16),
            pltpu.VMEM((2 * cols, KN * R), BF16),
            pltpu.VMEM((spans, M, cols), BF16),
            pltpu.VMEM((2, spans, KN, Z) + piece, BF16),
            pltpu.VMEM((spans, KN, Z) + piece, BF16),
            pltpu.VMEM((spans, 2) + piece, BF16),
            pltpu.VMEM((spans, 2) + piece, BF16),
            pltpu.VMEM((spans, 2, KN) + piece, BF16),
            pltpu.VMEM((spans, 2, KN) + piece, BF16),
            pltpu.VMEM((uses,) + piece, BF16),
            pltpu.VMEM((nseq, cap) + piece, BF16),
            dma((14,)),
            dma((nseq, 2)),
            dma((2, 2)),
            dma((nseq, 2)),
            dma((8, spans, 2)),
            dma((5, spans, 2)),
            dma((nseq, 2)),
            dma((2,)),
        ],
        compiler_params=pltpu.CompilerParams(
            collective_id=0, has_side_effects=True, vmem_limit_bytes=56 * 2**20
        ),
    )(
        neighbour_owner.T, neighbour_row.T, queries, out_grad, enc_table,
        key_weight.reshape(Z, 2, de_e, cols), value_weight.reshape(Z, 2, de_e, cols),
    )
    return pl.pallas_call(
        functools.partial(last_kernel, nseq, cap),
        out_shape=(
            jax.ShapeDtypeStruct((tok_rows, cols), BF16),
            jax.ShapeDtypeStruct((blocks,) + piece, F32),
        ),
        in_specs=[any_spec] * 4,
        out_specs=(any_spec,) * 2,
        scratch_shapes=[
            pltpu.SMEM((nseq, 1, 128), jnp.int32),
            pltpu.VMEM((nseq, cap) + piece, BF16),
            pltpu.VMEM((spans, M, cols), BF16),
            pltpu.VMEM((M, cols), BF16),
            pltpu.VMEM((tok_rows + M, cols), F32),
            pltpu.VMEM((tok_rows, cols), BF16),
            pltpu.VMEM((blocks,) + piece, F32),
            dma((6,)),
        ],
        compiler_params=pltpu.CompilerParams(vmem_limit_bytes=60 * 2**20),
    )(reqs, back, dq, prev)


def solution(mesh):
    in_specs = (
        P("seq", "enc"),
        P("seq", "enc"),
        P("seq", "enc", None),
        P(None, "enc"),
        P(None, "enc"),
        P("seq", None),
        P("seq", None),
    )
    out_specs = (P("seq", "enc"), P("seq", "enc", None))
    return jax.shard_map(local, mesh=mesh, in_specs=in_specs, out_specs=out_specs, check_vma=False)
```

```python
import functools
import math

import jax
import jax.numpy as jnp
from jax import lax
from jax.experimental import pallas as pl
from jax.experimental.pallas import tpu as pltpu
from jax.sharding import PartitionSpec as P

M = 64
KN = 2
R = 128
DE = 896
DH = 128
SEQ_LEN = 2048
Z = 4
MESH = pl.DeviceIdType.MESH
F32 = jnp.float32
BF16 = jnp.bfloat16


def dot(a, b):
    return jnp.dot(a, b, preferred_element_type=F32)


def dot_nt(a, b):
    return lax.dot_general(a, b, (((1,), (1,)), ((), ())), preferred_element_type=F32)


def main_kernel(
    nseq, cap, heads,
    own_h, row_h, q_h, g_h, tab_h, kw_h, vw_h,
    dq_o, prev_o, back_o, reqs_o,
    own_s, row_s, tab, qv, gv, wp, wt, qf, qs, gs, qt, gt, tails,
    req, uos, reqs, reqs_s, uos_s, slot_s,
    send_a, recv_a, gat, kvt, grad_t, dq,
    terms, sib_r, s1_s, s1_r, s2_s, s2_r, res, send_b,
    loc_sem, id_sem, tail_sem, a_sem, f_sem, b_sem, e_sem, dqt_sem,
):
    spans = qs.shape[0]
    uses = spans * KN
    de_e = tab.shape[1]
    cols = heads * DH
    scale = 1.0 / math.sqrt(DH)
    s = lax.axis_index("seq")
    e = lax.axis_index("enc")
    z, core = e // 2, e % 2
    zp, zm, zo = (z + 1) % Z, (z + 3) % Z, (z + 2) % Z
    sib = (s, z * 2 + 1 - core)
    up, down = (s, zp * 2 + core), (s, zm * 2 + core)
    per_seq = SEQ_LEN // (spans * M)
    ring = min(per_seq, nseq)
    base = (s // ring) * ring
    following = (base + (s + 1) % ring, e)
    preceding = (base + (s + ring - 1) % ring, e)

    def peer_of(i):
        i = 1 + (i + nseq // 2) % (nseq - 1)
        return ((s // ring + i // ring) % (nseq // ring)) * ring + (s % ring + i % ring) % ring

    def remote(src, dst, sem, where):
        return pltpu.make_async_remote_copy(
            src_ref=src, dst_ref=dst, send_sem=sem.at[0], recv_sem=sem.at[1],
            device_id=where, device_id_type=MESH,
        )

    barrier = pltpu.get_barrier_semaphore()

    def greet(i, _):
        pl.semaphore_signal(barrier, inc=1, device_id=(peer_of(i), e), device_id_type=MESH)
        return 0

    lax.fori_loop(1, nseq, greet, 0)
    for where in (sib, up, down):
        pl.semaphore_signal(barrier, inc=1, device_id=where, device_id_type=MESH)

    ids_in = [
        pltpu.make_async_copy(own_h, own_s, loc_sem.at[12]),
        pltpu.make_async_copy(row_h, row_s, loc_sem.at[13]),
    ]
    for c in ids_in:
        c.start()
    local = [
        pltpu.make_async_copy(tab_h, tab, loc_sem.at[0]),
        pltpu.make_async_copy(q_h, qv, loc_sem.at[1]),
        pltpu.make_async_copy(g_h, gv, loc_sem.at[2]),
        pltpu.make_async_copy(kw_h.at[:, core], wp.at[0, :, :, pl.ds(0, cols)], loc_sem.at[3]),
        pltpu.make_async_copy(vw_h.at[:, core], wp.at[0, :, :, pl.ds(cols, cols)], loc_sem.at[4]),
        pltpu.make_async_copy(kw_h.at[:, 1 - core], wp.at[1, :, :, pl.ds(0, cols)], loc_sem.at[5]),
        pltpu.make_async_copy(vw_h.at[:, 1 - core], wp.at[1, :, :, pl.ds(cols, cols)], loc_sem.at[6]),
    ]
    for c in local:
        c.start()

    for c in ids_in:
        c.wait()

    lane = lax.broadcasted_iota(jnp.int32, (1, 128), 1)
    lane_owner, lane_k = lane // cap, lane % cap
    count = jnp.zeros((1, 128), jnp.int32)
    rows = jnp.full((1, 128), -1, jnp.int32)
    use_of = jnp.zeros((1, 128), jnp.int32)
    owners = [own_s[u % KN, u // KN] for u in range(uses)]
    for u in range(uses):
        hit = lane_owner == owners[u]
        chosen = hit & (count == lane_k)
        rows = jnp.where(chosen, row_s[u % KN, u // KN], rows)
        use_of = jnp.where(chosen, u, use_of)
        count = count + hit.astype(jnp.int32)
        rank = jnp.int32(0)
        for v in range(u):
            rank = rank + (owners[v] == owners[u]).astype(jnp.int32)
        slot_s[u] = owners[u] * cap + rank
    req[...] = rows
    uos[...] = use_of
    reqs[s] = rows
    uos_copy = pltpu.make_async_copy(uos, uos_s, loc_sem.at[7])
    uos_copy.start()

    pl.semaphore_wait(barrier, nseq - 1 + 3)

    def id_copy(i):
        return remote(req, reqs.at[s], id_sem.at[i], (peer_of(i), e))

    def send_ids(i, _):
        id_copy(i).start()
        return 0

    lax.fori_loop(1, nseq, send_ids, 0)
    q_tail = remote(q_h.at[pl.ds(0, M)], tails.at[0], tail_sem.at[0], preceding)
    g_tail = remote(g_h.at[pl.ds(0, M)], tails.at[1], tail_sem.at[1], preceding)

    q_tail.start()
    g_tail.start()

    for c in local[3:]:
        c.wait()

    def turn(b, _):
        at = pl.ds(pl.multiple_of(b * 128, 128), 128)
        wt[at, :] = wp[:, :, :, at].reshape(DE, 128).T
        return 0

    lax.fori_loop(0, 2 * cols // 128, turn, 0)

    def shift(index, c):
        moved = qf[index, pl.ds(c * M + M - 1, M), :].astype(BF16)
        (qs, gs)[index][c] = moved
        (qt, gt)[index][c] = moved.T

    for index, source in enumerate((qv, gv)):
        local[1 + index].wait()
        qf[index, pl.ds(0, spans * M), :] = source[...].astype(F32)
        for c in range(spans - 1):
            shift(index, c)

    def wait_ids(i, _):
        id_copy(i).wait_recv()
        return 0

    lax.fori_loop(1, nseq, wait_ids, 0)
    reqs_copy = pltpu.make_async_copy(reqs, reqs_s, loc_sem.at[8])
    reqs_copy.start()
    reqs_out = pltpu.make_async_copy(reqs, reqs_o, loc_sem.at[9])
    reqs_out.start()
    local[0].wait()
    reqs_copy.wait()

    def a_copy(i):
        peer = peer_of(i)
        return remote(send_a.at[peer], recv_a.at[s], a_sem.at[i], (peer, e))

    def send_rows(i, _):
        peer = peer_of(i)
        for k in range(cap):
            wanted = jnp.maximum(reqs_s[peer, 0, s * cap + k], 0)
            send_a[peer, k] = tab[wanted]
        a_copy(i).start()
        return 0

    lax.fori_loop(1, nseq, send_rows, 0)
    for k in range(cap):
        recv_a[s, k] = tab[jnp.maximum(reqs_s[s, 0, s * cap + k], 0)]

    q_tail.wait_recv()
    g_tail.wait_recv()
    inside = jnp.logical_and(s % per_seq != per_seq - 1, s != nseq - 1).astype(F32)
    for index in range(2):
        qf[index, pl.ds(spans * M, M), :] = tails[index].astype(F32) * inside
        shift(index, spans - 1)
    uos_copy.wait()

    def wait_rows(i, _):
        a_copy(i).wait_recv()
        return 0

    lax.fori_loop(1, nseq, wait_rows, 0)

    def f_up(j):
        return remote(gat.at[j, :, 0, z], gat.at[j, :, 0, z], f_sem.at[0, j], up)

    def f_down(j):
        return remote(gat.at[j, :, 0, z], gat.at[j, :, 0, z], f_sem.at[1, j], down)

    def f_half_up(j):
        return remote(gat.at[j, 0, 0, zm], gat.at[j, 0, 0, zm], f_sem.at[2, j], up)

    def f_half_down(j):
        return remote(gat.at[j, 1, 0, zp], gat.at[j, 1, 0, zp], f_sem.at[3, j], down)

    def f_sib(j):
        return remote(gat.at[j, :, 0], gat.at[j, :, 1], f_sem.at[4, j], sib)

    def sibs(j):
        return [f_sib(j)]

    def b_sib(j):
        return remote(terms.at[1, j], sib_r.at[j], b_sem.at[0, j], sib)

    def b_one(j, d):
        return remote(s1_s.at[j, d], s1_r.at[j, d], b_sem.at[1 + d, j], (up, down)[d])

    def b_two(j, d):
        return remote(s2_s.at[j, d], s2_r.at[j, d], b_sem.at[3 + d, j], (up, down)[d])

    def forward_0(j):
        for t in range(KN):
            slot = slot_s[j * KN + t]
            gat[j, t, 0, z] = recv_a[slot // cap, slot % cap]
        f_up(j).start()
        f_down(j).start()

    def forward_1(j):
        f_up(j).wait_recv()
        f_half_up(j).start()
        f_down(j).wait_recv()
        f_half_down(j).start()

    def forward_2(j):
        f_half_up(j).wait_recv()
        f_half_down(j).wait_recv()
        f_sib(j).start()

    def forward_3(j):
        for c in sibs(j):
            c.wait_recv()

    def project(j):
        half = cols

        def some(b, _):
            at = pl.ds(pl.multiple_of(b * half, half), half)
            blocks = jnp.concatenate([gat[j, t].reshape(DE, R) for t in range(KN)], axis=1)
            kvt[at, :] = dot(wt[at, :], blocks).astype(BF16)
            return 0

        lax.fori_loop(0, 2, some, 0)

    def attend(j):
        hs = range(heads)
        at = [slice(h * DH, (h + 1) * DH) for h in hs]
        at_v = [slice(cols + h * DH, cols + (h + 1) * DH) for h in hs]
        scores = [dot(qs[j, :, at[h]], kvt[at[h], :]) * (scale * math.log2(math.e)) for h in hs]
        product = [dot(gs[j, :, at[h]], kvt[at_v[h], :]) for h in hs]
        powers = [jnp.exp2(x - jnp.max(x, axis=-1, keepdims=True)) for x in scores]
        weights = [x * (1.0 / jnp.sum(x, axis=-1, keepdims=True)) for x in powers]
        rounded = [x.astype(BF16) for x in weights]
        row_delta = [
            jnp.sum(x.astype(F32) * y, axis=-1, keepdims=True) for x, y in zip(rounded, product)
        ]
        score_grad = [(x * (y - d)).astype(BF16) for x, y, d in zip(weights, product, row_delta)]
        for h in hs:
            grad_t[at_v[h], :] = dot(gt[j, at[h], :], rounded[h]).astype(BF16)
        for h in hs:
            dq[j, :, at[h]] = (dot_nt(score_grad[h], kvt[at[h], :]) * scale).astype(BF16)
            grad_t[at[h], :] = (dot(qt[j, at[h], :], score_grad[h]) * scale).astype(BF16)
        for side in (1, 0):
            term = dot(wp[side].reshape(DE // 2, 2 * cols), grad_t[...]).astype(BF16)
            for t in range(KN):
                terms[side, j, t] = term[:, t * R:(t + 1) * R].reshape(Z, de_e, R)
            if side == 1:
                b_sib(j).start()

    def both(j, t, at):
        return terms[0, j, t, at].astype(F32) + sib_r[j, t, at].astype(F32)

    def backward_1(j):
        b_sib(j).wait_recv()
        s1_s[j, 0] = both(j, 0, zo).astype(BF16)
        b_one(j, 0).start()
        s1_s[j, 1] = both(j, 1, zo).astype(BF16)
        b_one(j, 1).start()

    def backward_2(j):
        for d, at in ((0, zp), (1, zm)):
            b_one(j, d).wait_recv()
            for t in range(KN):
                term = both(j, t, at)
                if t == d:
                    term = term + s1_r[j, d].astype(F32)
                s2_s[j, d, t] = term.astype(BF16)
            b_two(j, d).start()

    def backward_3(j):
        for d in range(2):
            b_two(j, d).wait_recv()
        for t in range(KN):
            term = both(j, t, z) + s2_r[j, 0, t].astype(F32) + s2_r[j, 1, t].astype(F32)
            res[j * KN + t] = term.astype(BF16)

    stages = ((0, forward_0), (4, forward_2), (2, forward_1), (5, forward_3), (5, project), (10, backward_3), (8, backward_2), (6, backward_1), (5, attend))

    def step(i, _):
        for offset, stage in stages:
            j = i - offset

            @pl.when(jnp.logical_and(j >= 0, j < spans))
            def _():
                stage(j)

        return 0

    lax.fori_loop(0, spans + 10, step, 0)

    dq_tail = remote(dq.at[spans - 1], prev_o, dqt_sem, following)
    dq_tail.start()
    dq_out = pltpu.make_async_copy(dq, dq_o, loc_sem.at[10])
    dq_out.start()

    def e_copy(i):
        peer = peer_of(i)
        return remote(send_b.at[peer], back_o.at[s], e_sem.at[i], (peer, e))

    def send_terms(i, _):
        peer = peer_of(i)
        for k in range(cap):
            send_b[peer, k] = res[uos_s[0, peer * cap + k]]
        e_copy(i).start()
        return 0

    lax.fori_loop(1, nseq, send_terms, 0)
    for k in range(cap):
        send_b[s, k] = res[uos_s[0, s * cap + k]]
    own_back = pltpu.make_async_copy(send_b.at[s], back_o.at[s], loc_sem.at[11])
    own_back.start()

    def drain(j, _):
        for c in [f_up(j), f_down(j), f_half_up(j), f_half_down(j)] + sibs(j):
            c.wait_send()
        for c in (b_sib(j), b_one(j, 0), b_one(j, 1), b_two(j, 0), b_two(j, 1)):
            c.wait_send()
        return 0

    lax.fori_loop(0, spans, drain, 0)

    def drain_peers(i, _):
        id_copy(i).wait_send()
        a_copy(i).wait_send()
        e_copy(i).wait()
        return 0

    lax.fori_loop(1, nseq, drain_peers, 0)
    q_tail.wait_send()
    g_tail.wait_send()
    dq_tail.wait()
    dq_out.wait()
    own_back.wait()
    reqs_out.wait()


def last_kernel(
    nseq, cap, reqs_h, back_h, dq_h, prev_h, dquery_o, dtable_o,
    reqs_s, back, dq, prev, shift, moved, total, sem,
):
    ins = [
        pltpu.make_async_copy(reqs_h, reqs_s, sem.at[0]),
        pltpu.make_async_copy(dq_h, dq, sem.at[1]),
        pltpu.make_async_copy(prev_h, prev, sem.at[2]),
        pltpu.make_async_copy(back_h, back, sem.at[3]),
    ]
    for c in ins:
        c.start()
    total[...] = jnp.zeros_like(total)
    s = lax.axis_index("seq")
    rows = dquery_o.shape[0]
    per_seq = SEQ_LEN // rows
    ins[1].wait()
    ins[2].wait()
    shift[pl.ds(0, M), :] = prev[...].astype(F32) * (s % per_seq != 0).astype(F32)
    shift[pl.ds(M, rows), :] = dq[...].reshape(rows, dq.shape[2]).astype(F32)
    moved[...] = shift[pl.ds(1, rows), :].astype(BF16)
    query_out = pltpu.make_async_copy(moved, dquery_o, sem.at[5])
    query_out.start()
    ins[0].wait()
    ins[3].wait()

    def add(i, _):
        row = reqs_s[i // cap, 0, s * cap + i % cap]

        @pl.when(row >= 0)
        def _():
            total[row] += back[i // cap, i % cap].astype(F32)

        return 0

    lax.fori_loop(0, nseq * cap, add, 0)
    table_out = pltpu.make_async_copy(total, dtable_o, sem.at[4])
    table_out.start()
    table_out.wait()
    query_out.wait()


def local(queries, out_grad, enc_table, key_weight, value_weight, neighbour_owner, neighbour_row):
    nseq = lax.axis_size("seq")
    tok_rows, cols = queries.shape
    heads = cols // DH
    spans = tok_rows // M
    uses = spans * KN
    cap = max(2, uses // nseq)
    blocks, de_e, _ = enc_table.shape
    any_spec = pl.BlockSpec(memory_space=pl.ANY)
    piece = (de_e, R)
    dma = pltpu.SemaphoreType.DMA
    dq, prev, back, reqs = pl.pallas_call(
        functools.partial(main_kernel, nseq, cap, heads),
        out_shape=(
            jax.ShapeDtypeStruct((spans, M, cols), BF16),
            jax.ShapeDtypeStruct((M, cols), BF16),
            jax.ShapeDtypeStruct((nseq, cap) + piece, BF16),
            jax.ShapeDtypeStruct((nseq, 1, 128), jnp.int32),
        ),
        in_specs=[any_spec] * 7,
        out_specs=(any_spec,) * 4,
        scratch_shapes=[
            pltpu.SMEM((KN, spans), jnp.int32),
            pltpu.SMEM((KN, spans), jnp.int32),
            pltpu.VMEM((blocks,) + piece, BF16),
            pltpu.VMEM((tok_rows, cols), BF16),
            pltpu.VMEM((tok_rows, cols), BF16),
            pltpu.VMEM((2, Z, de_e, 2 * cols), BF16),
            pltpu.VMEM((2 * cols, DE), BF16),
            pltpu.VMEM((2, tok_rows + M, cols), F32),
            pltpu.VMEM((spans, M, cols), BF16),
            pltpu.VMEM((spans, M, cols), BF16),
            pltpu.VMEM((spans, cols, M), BF16),
            pltpu.VMEM((spans, cols, M), BF16),
            pltpu.VMEM((2, M, cols), BF16),
            pltpu.VMEM((1, 128), jnp.int32),
            pltpu.VMEM((1, 128), jnp.int32),
            pltpu.VMEM((nseq, 1, 128), jnp.int32),
            pltpu.SMEM((nseq, 1, 128), jnp.int32),
            pltpu.SMEM((1, 128), jnp.int32),
            pltpu.SMEM((uses,), jnp.int32),
            pltpu.VMEM((nseq, cap) + piece, BF16),
            pltpu.VMEM((nseq, cap) + piece, BF16),
            pltpu.VMEM((spans, KN, 2, Z) + piece, BF16),
            pltpu.VMEM((2 * cols, KN * R), BF16),
            pltpu.VMEM((2 * cols, KN * R), BF16),
            pltpu.VMEM((spans, M, cols), BF16),
            pltpu.VMEM((2, spans, KN, Z) + piece, BF16),
            pltpu.VMEM((spans, KN, Z) + piece, BF16),
            pltpu.VMEM((spans, 2) + piece, BF16),
            pltpu.VMEM((spans, 2) + piece, BF16),
            pltpu.VMEM((spans, 2, KN) + piece, BF16),
            pltpu.VMEM((spans, 2, KN) + piece, BF16),
            pltpu.VMEM((uses,) + piece, BF16),
            pltpu.VMEM((nseq, cap) + piece, BF16),
            dma((14,)),
            dma((nseq, 2)),
            dma((2, 2)),
            dma((nseq, 2)),
            dma((8, spans, 2)),
            dma((5, spans, 2)),
            dma((nseq, 2)),
            dma((2,)),
        ],
        compiler_params=pltpu.CompilerParams(
            collective_id=0, has_side_effects=True, vmem_limit_bytes=56 * 2**20
        ),
    )(
        neighbour_owner.T, neighbour_row.T, queries, out_grad, enc_table,
        key_weight.reshape(Z, 2, de_e, cols), value_weight.reshape(Z, 2, de_e, cols),
    )
    return pl.pallas_call(
        functools.partial(last_kernel, nseq, cap),
        out_shape=(
            jax.ShapeDtypeStruct((tok_rows, cols), BF16),
            jax.ShapeDtypeStruct((blocks,) + piece, F32),
        ),
        in_specs=[any_spec] * 4,
        out_specs=(any_spec,) * 2,
        scratch_shapes=[
            pltpu.SMEM((nseq, 1, 128), jnp.int32),
            pltpu.VMEM((nseq, cap) + piece, BF16),
            pltpu.VMEM((spans, M, cols), BF16),
            pltpu.VMEM((M, cols), BF16),
            pltpu.VMEM((tok_rows + M, cols), F32),
            pltpu.VMEM((tok_rows, cols), BF16),
            pltpu.VMEM((blocks,) + piece, F32),
            dma((6,)),
        ],
        compiler_params=pltpu.CompilerParams(vmem_limit_bytes=60 * 2**20),
    )(reqs, back, dq, prev)


def solution(mesh):
    in_specs = (
        P("seq", "enc"),
        P("seq", "enc"),
        P("seq", "enc", None),
        P(None, "enc"),
        P(None, "enc"),
        P("seq", None),
        P("seq", None),
    )
    out_specs = (P("seq", "enc"), P("seq", "enc", None))
    return jax.shard_map(local, mesh=mesh, in_specs=in_specs, out_specs=out_specs, check_vma=False)
```
